32 devices in a mesh: dp: 4 (over x, core), fsdp: 8 (over z, y).
Axes of the slice: x: 2, y: 2, z: 4, core: 2. Of those that a mesh axis runs over, the one named last changes fastest.
Arguments:
- inputs: bfloat16 [2, 4096, 1536], P(None, ('dp', 'fsdp')), may hold values from -6 to 6
- documents: int32 [2, 32, 128], P(None, ('dp', 'fsdp')), may hold values from 0 to 1, never falling along the last dimension, each value on 1 to 96 neighbouring positions
- out_grad: bfloat16 [2, 4096, 1536], P(None, ('dp', 'fsdp')), may hold values from -6 to 6
- query_weight: bfloat16 [1536, 1536], P(('dp', 'fsdp')), may hold values from -0.15625 to 0.15625
- key_weight: bfloat16 [1536, 1536], P(('dp', 'fsdp')), may hold values from -0.15625 to 0.15625
- value_weight: bfloat16 [1536, 1536], P(('dp', 'fsdp')), may hold values from -0.15625 to 0.15625
- outgate_weight: bfloat16 [1536, 1536], P(('dp', 'fsdp')), may hold values from -0.15625 to 0.15625
- output_weight: bfloat16 [1536, 1536], P(('dp', 'fsdp')), may hold values from -0.4375 to 0.4375
- forget_weight: bfloat16 [1536, 24], P(('dp', 'fsdp')), may hold values from -0.15625 to 0.15625
- forget_bias: float32 [24], replicated, may hold values from 0 to 6
- gains: bfloat16 [1536, 4], P(('dp', 'fsdp')), may hold values from 0.5 to 1.5
- swiglu_gate: bfloat16 [1536, 4096], P(('dp', 'fsdp')), may hold values from -0.15625 to 0.15625
- swiglu_up: bfloat16 [1536, 4096], P(('dp', 'fsdp')), may hold values from -0.15625 to 0.15625
- swiglu_down: bfloat16 [4096, 1536], P(('dp', 'fsdp')), may hold values from -0.1875 to 0.1875
Outputs:
- outputs: bfloat16 [2, 4096, 1536], P(None, ('dp', 'fsdp'))
- input_grad: bfloat16 [2, 4096, 1536], P(None, ('dp', 'fsdp'))
- query_grad: float32 [1536, 1536], P(('dp', 'fsdp'))
- key_grad: float32 [1536, 1536], P(('dp', 'fsdp'))
- value_grad: float32 [1536, 1536], P(('dp', 'fsdp'))
- outgate_grad: float32 [1536, 1536], P(('dp', 'fsdp'))
- output_grad: float32 [1536, 1536], P(('dp', 'fsdp'))
- forget_grad: float32 [1536, 24], P(('dp', 'fsdp'))
- bias_grad: float32 [24], replicated
- gains_grad: float32 [1536, 4], P(('dp', 'fsdp'))
- gate_grad: float32 [1536, 4096], P(('dp', 'fsdp'))
- up_grad: float32 [1536, 4096], P(('dp', 'fsdp'))
- down_grad: float32 [4096, 1536], P(('dp', 'fsdp'))
The draws below stay inside these ranges and needn't reach their ends.
Inputs may be any that keep to these rules, and one draw needn't show every extreme that they name: Along a device's tokens of one micro-batch the document number never falls; a document has 1 to 96 tokens there, so a device's block holds one or two documents.
All inputs are finite; a program needn't handle non-finite values.
Results may differ from the reference program's by a relative error of at most 0.015.
Values may be sent and summed in bfloat16 or wider, within the bound.
A program may use at most 256 MiB of HBM per device.

```python
import math
import jax
import jax.numpy as jnp
import numpy as np
from jax import lax

D = 1536
HEADS = 24
HEAD_DIM = 64
FF = 4096
ROW_DEV = 128
MB = 2
DOCS = 2
DOC_MOST = 96
ROWS = 4096
DEVICES = 32


def steps_of(stream_key, dims, shards, low, largest):
    loudness, own = 1.0, jax.random.fold_in(stream_key, 6)
    for dim, parts in shards:
        draws = jnp.exp(jax.random.uniform(jax.random.fold_in(own, dim), (parts,), jnp.float32, low / len(shards), largest / len(shards)))
        loudness = loudness * jnp.repeat(draws, dims[dim] // parts).reshape([-1 if axis == dim else 1 for axis in range(len(dims))])
    return loudness


def length_profile(number_of, total, most, slope):
    weights = [(1 << 20) // math.isqrt(rank ** slope) + 1 for rank in range(2, number_of + 1)]
    surplus, counts = total - most - (number_of - 1), [1] * (number_of - 1)
    while surplus > 0:
        free = [i for i in range(number_of - 1) if counts[i] < most]
        mass, budget = sum([weights[i] for i in free]), surplus
        for i in free:
            extra = min(most - counts[i], max(1, budget * weights[i] // mass), surplus)
            counts[i] = counts[i] + extra
            surplus = surplus - extra
    return np.array([most] + counts)


def ragged(rng, number_of, total, bound, lean):
    if number_of == 2:
        one = jax.random.randint(rng, (), max(1, total - bound), min(bound, total - 1) + 1)
        return jnp.stack([one, total - one])
    lengths = jnp.asarray(length_profile(number_of, total, bound, lean), jnp.int32)
    twos = (number_of - 1) // 2
    source_of, receiver = lengths[1:1 + 2 * twos:2], lengths[2:2 + 2 * twos:2]
    slack = jnp.minimum(source_of - 1, bound - receiver)
    moved = jax.random.randint(jax.random.fold_in(rng, 1), (twos,), 0, 1 << 20) % (slack + 1)
    lengths = lengths.at[1:1 + 2 * twos:2].set(source_of - moved).at[2:2 + 2 * twos:2].set(receiver + moved)
    return lengths[jax.random.permutation(jax.random.fold_in(rng, 2), number_of)]


def normal_values(key, shape, width, bound, pieces=(), kind=jnp.bfloat16):
    array = width * jax.random.normal(key, shape, jnp.float32)
    if pieces:
        array = array * steps_of(key, shape, pieces, -0.22, 0.18)
    return jnp.clip(array, -bound, bound).astype(kind)


def setup_inputs(seed: int = 0) -> dict:
    seeds = jax.random.split(jax.random.key(seed), 15)
    return {
        "inputs": normal_values(seeds[0], (MB, ROWS, D), 1.0, 6.0, ((1, 32),)),
        "documents": jax.vmap(lambda own: jnp.searchsorted(jnp.cumsum(ragged(own, DOCS, ROW_DEV, DOC_MOST, 0)), jnp.arange(ROW_DEV), side="right"))(jax.random.split(seeds[1], MB * DEVICES)).reshape((MB, DEVICES, ROW_DEV)).astype(jnp.int32),
        "out_grad": normal_values(seeds[2], (MB, ROWS, D), 1.0, 6.0, ((1, 32),)),
        "query_weight": normal_values(seeds[3], (D, D), D ** -0.5, 0.15625, ((0, 32),)),
        "key_weight": normal_values(seeds[4], (D, D), D ** -0.5, 0.15625, ((0, 32),)),
        "value_weight": normal_values(seeds[5], (D, D), D ** -0.5, 0.15625, ((0, 32),)),
        "outgate_weight": normal_values(seeds[6], (D, D), D ** -0.5, 0.15625, ((0, 32),)),
        "output_weight": normal_values(seeds[7], (D, D), (D // 8) ** -0.5, 0.4375, ((0, 32),)),
        "forget_weight": normal_values(seeds[8], (D, HEADS), D ** -0.5, 0.15625, ((0, 32),)),
        "forget_bias": jnp.clip(jax.random.uniform(seeds[9], (HEADS,), jnp.float32, 0.0, 6.0), 0.0, 6.0),
        "gains": jnp.clip(1.0 + 0.1 * jax.random.normal(seeds[10], (D, 4), jnp.float32), 0.5, 1.5).astype(jnp.bfloat16),
        "swiglu_gate": normal_values(seeds[11], (D, FF), D ** -0.5, 0.15625, ((0, 32),)),
        "swiglu_up": normal_values(seeds[12], (D, FF), D ** -0.5, 0.15625, ((0, 32),)),
        "swiglu_down": normal_values(seeds[13], (FF, D), (FF // 4) ** -0.5, 0.1875, ((0, 32),)),
    }


@jax.custom_vjp
def low(v):
    return lax.optimization_barrier(v.astype(jnp.bfloat16)).astype(jnp.float32)

@jax.custom_vjp
def low_back(v):
    return v

def low_keep(v):
    return (low(v), None)

def low_pass(kept, grad):
    return (grad,)

def back_keep(v):
    return (v, None)

def back_low(kept, grad):
    return (low(grad),)
low.defvjp(low_keep, low_pass)
low_back.defvjp(back_keep, back_low)
EPSILON = 1e-06
HIGHEST = lax.Precision.HIGHEST

def matmul(left_side, right_side):
    return jnp.dot(left_side, right_side, precision=HIGHEST)

def rms_norm(tensor, gain_row):
    return tensor * lax.rsqrt(lax.optimization_barrier(jnp.mean(tensor * tensor, axis=-1, keepdims=True)) + EPSILON) * gain_row

def layer_rows(weights, row_block, doc_ids):
    query_w, key_w, value_w, ogate_w, output_w, forget_w, forget_b, gain_cols, gate_w, up_w, down_w = weights
    row_count = row_block.shape[0]
    hidden_one = low(rms_norm(row_block, gain_cols[:, 0]))
    queries = low_back(matmul(hidden_one, query_w)).reshape(row_count, HEADS, HEAD_DIM)
    keys_raw = low_back(matmul(hidden_one, key_w)).reshape(row_count, HEADS, HEAD_DIM)
    values = low(low_back(matmul(hidden_one, value_w))).reshape(row_count, HEADS, HEAD_DIM)
    gate_pre = low_back(matmul(hidden_one, ogate_w))
    forget_pre = low_back(matmul(hidden_one, forget_w) + forget_b)
    query_n = low(rms_norm(queries, gain_cols[:, 1].reshape(HEADS, HEAD_DIM)))
    key_n = low(rms_norm(keys_raw, gain_cols[:, 2].reshape(HEADS, HEAD_DIM)))
    decay = jnp.cumsum(jax.nn.log_sigmoid(forget_pre), axis=0).T
    scores = jnp.einsum('ihd,jhd->hij', query_n, key_n, precision=HIGHEST) / math.sqrt(HEAD_DIM)
    scores = low_back(scores + decay[:, :, None] - decay[:, None, :])
    positions = jnp.arange(row_count)
    allowed = (doc_ids[:, None] == doc_ids[None, :]) & (positions[None, :] <= positions[:, None])
    scores = jnp.where(allowed[None], scores, -1e+30)
    row_max = lax.optimization_barrier(jnp.max(scores, axis=-1, keepdims=True))
    shifted = jnp.exp(scores - row_max)
    probs = low(shifted / lax.optimization_barrier(jnp.sum(shifted, axis=-1, keepdims=True)))
    attended = low_back(jnp.einsum('hij,jhd->ihd', probs, values, precision=HIGHEST)).reshape(row_count, D)
    gated = low(attended * jax.nn.sigmoid(gate_pre))
    middle = row_block + low_back(matmul(gated, output_w))
    hidden_two = low(rms_norm(middle, gain_cols[:, 3]))
    gate_act = low_back(matmul(hidden_two, gate_w))
    up_act = low_back(matmul(hidden_two, up_w))
    activated = low(jax.nn.silu(gate_act) * up_act)
    return middle + low_back(matmul(activated, down_w))

def reference(inputs, documents, out_grad, query_weight, key_weight, value_weight, outgate_weight, output_weight, forget_weight, forget_bias, gains, swiglu_gate, swiglu_up, swiglu_down):
    weights = (query_weight.astype(jnp.float32), key_weight.astype(jnp.float32), value_weight.astype(jnp.float32), outgate_weight.astype(jnp.float32), output_weight.astype(jnp.float32), forget_weight.astype(jnp.float32), forget_bias.astype(jnp.float32), gains.astype(jnp.float32), swiglu_gate.astype(jnp.float32), swiglu_up.astype(jnp.float32), swiglu_down.astype(jnp.float32))
    block_count = MB * DEVICES
    all_rows = inputs.astype(jnp.float32).reshape(block_count, ROW_DEV, D)
    all_docs = documents.reshape(block_count, ROW_DEV)

    def forward(weight_set, row_blocks):

        def one_block(item):
            return layer_rows(weight_set, item[0], item[1])
        return lax.map(jax.checkpoint(one_block), (row_blocks, all_docs))
    result, pullback = jax.vjp(forward, weights, all_rows)
    weight_grads, rows_grad = pullback(out_grad.astype(jnp.float32).reshape(block_count, ROW_DEV, D))
    return (result.reshape(MB, ROWS, D).astype(jnp.bfloat16), rows_grad.reshape(MB, ROWS, D).astype(jnp.bfloat16), weight_grads[0], weight_grads[1], weight_grads[2], weight_grads[3], weight_grads[4], weight_grads[5], weight_grads[6], weight_grads[7], weight_grads[8], weight_grads[9], weight_grads[10])
```

```python
import math

import jax
import jax.numpy as jnp
import numpy as np
from jax import lax
from jax.sharding import PartitionSpec as P

EPSILON = 1e-06
BOTH = ("dp", "fsdp")
F32 = jnp.float32
BF16 = jnp.bfloat16


def rms_scale(tensor):
    return lax.rsqrt(jnp.mean(tensor * tensor, axis=-1, keepdims=True) + EPSILON)


def norm_back(grad_normed, normed, scale):
    return scale * (grad_normed - normed * jnp.mean(grad_normed * normed, axis=-1, keepdims=True))


def product(left_side, right_side):
    return jnp.dot(left_side, right_side, preferred_element_type=F32)


def product_tn(left_side, right_side):
    return lax.dot_general(
        left_side, right_side, (((0,), (0,)), ((), ())), preferred_element_type=F32
    )


def product_nt(left_side, right_side):
    return lax.dot_general(
        left_side, right_side, (((1,), (1,)), ((), ())), preferred_element_type=F32
    )


class Place:
    def __init__(self, mesh):
        self.dp = mesh.shape["dp"]
        self.fsdp = mesh.shape["fsdp"]
        self.zs = self.fsdp // 2
        self.core = self.perm(lambda x, c, z, y: (x, 1 - c, z, y))
        self.over_x = self.perm(lambda x, c, z, y: (1 - x, c, z, y))
        self.over_y = self.perm(lambda x, c, z, y: (x, c, z, 1 - y))
        self.over_xc = self.perm(lambda x, c, z, y: (1 - x, 1 - c, z, y))
        self.over_yc = self.perm(lambda x, c, z, y: (x, 1 - c, z, 1 - y))
        self.swap_xy = self.perm(lambda x, c, z, y: (y, c, z, x))
        order = []
        for z in range(self.zs):
            offs = sorted((j - z for j in range(self.zs)), key=lambda o: (abs(o), o if z % 2 else -o))
            order.append(offs)
        self.slots = [[order[z][t] for z in range(self.zs)] for t in range(self.zs)]

    def index(self, x, c, z, y):
        return (x * 2 + c) * self.fsdp + z * 2 + y

    def perm(self, target):
        pairs = []
        for x in range(2):
            for c in range(2):
                for z in range(self.zs):
                    for y in range(2):
                        to = target(x, c, z, y)
                        if to is not None:
                            pairs.append((self.index(x, c, z, y), self.index(*to)))
        return pairs

    def along(self, sign, hops):
        def target(x, c, z, y):
            back, to = z - sign * (hops - 1), z + sign
            if 0 <= back < self.zs and 0 <= to < self.zs:
                return (x, c, to, y)
            return None

        return self.perm(target)

    def toward(self, sign, offset):
        def target(x, c, z, y):
            if 0 <= z + sign * offset < self.zs:
                return (x, c, z + sign, y)
            return None

        return self.perm(target)


def send(value, perm):
    return lax.ppermute(value, BOTH, perm)


def pick(which, options):
    first = options[0]
    if all(option is first for option in options):
        return first
    return lax.select_n(which, *options)


def local(
    place,
    inputs,
    documents,
    out_grad,
    query_weight,
    key_weight,
    value_weight,
    outgate_weight,
    output_weight,
    forget_weight,
    forget_bias,
    gains,
    swiglu_gate,
    swiglu_up,
    swiglu_down,
):
    head_total = forget_weight.shape[1]
    micro_count, row_count, width = inputs.shape
    head_width = width // head_total
    heads = head_total // 4
    own_rows = query_weight.shape[0]
    part = width // 4
    hidden = swiglu_gate.shape[1] // 4
    zs = place.zs
    score_root = math.sqrt(head_width)
    positions = jnp.arange(row_count)

    dp_at = lax.axis_index("dp")
    fsdp_at = lax.axis_index("fsdp")
    x_at, c_at = dp_at // 2, dp_at % 2
    z_at, y_at = fsdp_at // 2, fsdp_at % 2
    at_y = y_at * 2 + c_at
    at_x = x_at * 2 + c_at

    def group_gather(value, across):
        there = send(value, across)
        return [value, there, send(value, place.core), send(there, place.core)]

    def group_sum(parts, across):
        core_own = send(parts[2].astype(BF16), place.core).astype(F32)
        core_across = send(parts[3].astype(BF16), place.core).astype(F32)
        over = send((parts[1] + core_across).astype(BF16), across).astype(F32)
        return parts[0] + core_own + over

    def exchange(blocks, at, perms):
        kept = [blocks(at ^ rel) for rel in range(4)]
        came = [kept[0]] + [send(kept[rel], perms[rel]) for rel in (1, 2, 3)]
        return [pick(at, [came[member ^ own] for own in range(4)]) for member in range(4)]

    y_perms = (None, place.core, place.over_y, place.over_yc)
    x_perms = (None, place.core, place.over_x, place.over_xc)

    def unit_gather(unit, across, across_at):
        near = {0: unit}
        right = left = unit
        for step in range(1, zs):
            right = send(right, place.along(1, step))
            left = send(left, place.along(-1, step))
            near[-step], near[step] = right, left
        crossed = []
        for slot in range(zs):
            chosen = pick(z_at, [near[place.slots[slot][z]] for z in range(zs)])
            crossed.append(send(chosen, across))
        rows = []
        for owner in range(zs):
            own = pick(z_at, [near[owner - z] for z in range(zs)])
            over = pick(
                z_at,
                [crossed[[place.slots[s][z] for s in range(zs)].index(owner - z)] for z in range(zs)],
            )
            rows.append([jnp.where(across_at == 0, own, over), jnp.where(across_at == 0, over, own)])
        return rows

    def unit_sum(blocks, across, across_at):
        summed = [None] * zs
        mine = lax.dynamic_index_in_dim(blocks, across_at, 1, keepdims=False)
        other = lax.dynamic_index_in_dim(blocks, 1 - across_at, 1, keepdims=False)
        for slot in reversed(range(zs)):
            owner = z_at + jnp.asarray(np.array(place.slots[slot], np.int32))[z_at]
            gone = lax.dynamic_index_in_dim(other, owner, 0, keepdims=False).astype(BF16)
            came = send(gone, across).astype(F32)
            summed[slot] = came + lax.dynamic_index_in_dim(mine, owner, 0, keepdims=False).astype(F32)

        def at_offset(offset):
            options = []
            for z in range(zs):
                offs = [place.slots[s][z] for s in range(zs)]
                options.append(summed[offs.index(offset)] if offset in offs else summed[0])
            return pick(z_at, options)

        total = summed[0]
        for sign in (1, -1):
            carried = None
            for offset in range(zs - 1, 0, -1):
                term = at_offset(sign * offset)
                if carried is not None:
                    term = term + carried
                carried = send(term.astype(BF16), place.toward(sign, offset)).astype(F32)
            total = total + carried
        return total

    small = lax.all_gather(
        jnp.concatenate([forget_weight, gains], axis=1), BOTH, axis=0, tiled=True
    )
    docs_all = [d[:, 0] for d in group_gather(documents, place.over_y)]
    rows_y = group_gather(inputs, place.over_y)

    attn_blocks = jnp.concatenate(
        [w.reshape(own_rows, 4, part) for w in (query_weight, key_weight, value_weight, outgate_weight)],
        axis=2,
    )
    attn_unit = jnp.stack(
        exchange(
            lambda j: lax.dynamic_index_in_dim(attn_blocks, j, 1, keepdims=False), at_y, y_perms
        )
    )
    attn_all = unit_gather(attn_unit, place.over_x, x_at)
    out_unit = send(output_weight, place.swap_xy)
    out_all = unit_gather(out_unit, place.over_x, x_at)
    ffn_blocks = jnp.concatenate(
        [w.reshape(own_rows, 4, hidden) for w in (swiglu_gate, swiglu_up)], axis=2
    )
    ffn_unit = jnp.stack(
        exchange(
            lambda j: lax.dynamic_index_in_dim(ffn_blocks, j, 1, keepdims=False), at_x, x_perms
        )
    )
    ffn_all = unit_gather(ffn_unit, place.over_y, y_at)
    down_all = unit_gather(swiglu_down, place.over_y, y_at)
    dy_x = group_gather(out_grad, place.over_x)

    def rows_from(units, first, columns):
        stacked = jnp.stack([jnp.stack(u) for u in units]).reshape(zs, 2, 2, 2, own_rows, columns)
        return stacked

    attn_w = (
        rows_from(attn_all, 0, 4 * part).transpose(1, 3, 0, 2, 4, 5).reshape(width, 4 * part)
    )
    ffn_w = (
        rows_from(ffn_all, 0, 2 * hidden).transpose(2, 3, 0, 1, 4, 5).reshape(width, 2 * hidden)
    )
    out_w = jnp.concatenate([v for u in out_all for v in u], axis=0)
    down_w = jnp.concatenate([v for u in down_all for v in u], axis=0)

    forget_all = small[:, :head_total]
    gain_cols = small[:, head_total:].astype(F32)
    forget_w = lax.dynamic_slice_in_dim(forget_all, at_y * heads, heads, 1)
    forget_b = lax.dynamic_slice_in_dim(forget_bias, at_y * heads, heads, 0)
    query_gain = lax.dynamic_slice_in_dim(gain_cols[:, 1], at_y * part, part).reshape(heads, head_width)
    key_gain = lax.dynamic_slice_in_dim(gain_cols[:, 2], at_y * part, part).reshape(heads, head_width)

    def split_heads(value):
        return value.reshape(4, row_count, heads, head_width)

    def join_heads(value):
        return value.reshape(4 * row_count, part)

    def scores_of(query_n, key_n, decay, allowed):
        scores = (
            jnp.einsum("bihd,bjhd->bhij", query_n, key_n, preferred_element_type=F32) / score_root
        )
        scores = scores + decay[:, :, :, None] - decay[:, :, None, :]
        return jnp.where(allowed[:, None], scores, -1e30)

    kept = []
    for m in range(micro_count):
        k = {}
        doc_ids = jnp.stack([d[m] for d in docs_all])
        allowed = (doc_ids[:, :, None] == doc_ids[:, None, :]) & (
            positions[None, None, :] <= positions[None, :, None]
        )
        group_rows = jnp.concatenate([v[m] for v in rows_y]).astype(F32)
        hidden_one = (group_rows * rms_scale(group_rows) * gain_cols[:, 0]).astype(BF16)
        mixed = product(hidden_one, attn_w)
        queries = split_heads(mixed[:, :part])
        keys_raw = split_heads(mixed[:, part : 2 * part])
        values_low = split_heads(mixed[:, 2 * part : 3 * part].astype(BF16))
        gate_pre = mixed[:, 3 * part :]
        forget_pre = (product(hidden_one, forget_w) + forget_b).reshape(4, row_count, heads)
        query_scale = rms_scale(queries)
        query_hat = queries * query_scale
        query_n = (query_hat * query_gain).astype(BF16)
        key_scale = rms_scale(keys_raw)
        key_hat = keys_raw * key_scale
        key_n = (key_hat * key_gain).astype(BF16)
        decay = jnp.cumsum(jax.nn.log_sigmoid(forget_pre), axis=1).transpose(0, 2, 1)
        scores = scores_of(query_n, key_n, decay, allowed)
        row_max = jnp.max(scores, axis=-1, keepdims=True)
        shifted = jnp.exp(scores - row_max)
        row_total = jnp.sum(shifted, axis=-1, keepdims=True)
        log_total = row_max + jnp.log(row_total)
        probs_low = (shifted / row_total).astype(BF16)
        attended = join_heads(
            jnp.einsum("bhij,bjhd->bihd", probs_low, values_low, preferred_element_type=F32)
        )
        gate_sig = jax.nn.sigmoid(gate_pre)
        gated = (attended * gate_sig).astype(BF16)
        partial = product(gated, out_w).reshape(4, row_count, width)
        rows_own = inputs[m].astype(F32)
        middle = rows_own + group_sum([partial[i] for i in range(4)], place.over_y)
        scale_two = rms_scale(middle)
        normed_two = middle * scale_two
        hidden_own = (normed_two * gain_cols[:, 3]).astype(BF16)
        hidden_two = jnp.concatenate(group_gather(hidden_own, place.over_x))
        acts = product(hidden_two, ffn_w)
        gate_act, up_act = acts[:, :hidden], acts[:, hidden:]
        gate_sg = jax.nn.sigmoid(gate_act)
        activated = (gate_act * gate_sg * up_act).astype(BF16)
        down_in = jnp.concatenate([v[m] for v in dy_x])
        partial = product(activated, down_w).reshape(4, row_count, width)
        k["result"] = (middle + group_sum([partial[i] for i in range(4)], place.over_x)).astype(BF16)
        grad_act = product_nt(down_in, down_w)
        grad_gate = (grad_act * up_act * gate_sg * (1.0 + gate_act * (1.0 - gate_sg))).astype(BF16)
        grad_upact = (grad_act * gate_act * gate_sg).astype(BF16)
        grad_both = jnp.concatenate([grad_gate, grad_upact], axis=1)
        partial = product_nt(grad_both, ffn_w).reshape(4, row_count, width)
        grad_hidden_two = group_sum([partial[i] for i in range(4)], place.over_x)
        upstream = out_grad[m].astype(F32)
        k["gain_three"] = jnp.sum(grad_hidden_two * normed_two, axis=0)
        grad_middle = upstream + norm_back(grad_hidden_two * gain_cols[:, 3], normed_two, scale_two)
        output_in = jnp.concatenate(group_gather(grad_middle.astype(BF16), place.over_y))
        k["ffn"] = (activated, down_in, hidden_two, grad_both)
        grad_gated = product_nt(output_in, out_w)
        grad_attended = split_heads((grad_gated * gate_sig).astype(BF16))
        grad_gatepre = (grad_gated * attended * gate_sig * (1.0 - gate_sig)).astype(BF16)
        probs = jnp.exp(scores_of(query_n, key_n, decay, allowed) - log_total)
        grad_probs = jnp.einsum("bihd,bjhd->bhij", grad_attended, values_low, preferred_element_type=F32)
        grad_values = jnp.einsum(
            "bhij,bihd->bjhd", probs.astype(BF16), grad_attended, preferred_element_type=F32
        )
        grad_scores = (
            probs * (grad_probs - jnp.sum(probs * grad_probs, axis=-1, keepdims=True))
        ).astype(BF16)
        grad_query_n = (
            jnp.einsum("bhij,bjhd->bihd", grad_scores, key_n, preferred_element_type=F32) / score_root
        )
        grad_key_n = (
            jnp.einsum("bhij,bihd->bjhd", grad_scores, query_n, preferred_element_type=F32) / score_root
        )
        scores_wide = grad_scores.astype(F32)
        grad_decay = (jnp.sum(scores_wide, axis=3) - jnp.sum(scores_wide, axis=2)).transpose(0, 2, 1)
        grad_logf = jnp.flip(jnp.cumsum(jnp.flip(grad_decay, 1), axis=1), 1)
        grad_forget = (
            (grad_logf * (1.0 - jax.nn.sigmoid(forget_pre))).astype(BF16).reshape(4 * row_count, heads)
        )
        k["bias"] = jnp.sum(grad_forget.astype(F32), axis=0)
        k["gain_query"] = jnp.sum(grad_query_n * query_hat, axis=(0, 1)).reshape(part)
        k["gain_key"] = jnp.sum(grad_key_n * key_hat, axis=(0, 1)).reshape(part)
        grad_query = join_heads(
            norm_back(grad_query_n * query_gain, query_hat, query_scale).astype(BF16)
        )
        grad_key = join_heads(norm_back(grad_key_n * key_gain, key_hat, key_scale).astype(BF16))
        grad_value = join_heads(grad_values.astype(BF16))
        grad_mixed = jnp.concatenate([grad_query, grad_key, grad_value, grad_gatepre], axis=1)
        partial = (product_nt(grad_mixed, attn_w) + product_nt(grad_forget, forget_w)).reshape(
            4, row_count, width
        )
        grad_hidden_one = group_sum([partial[i] for i in range(4)], place.over_y)
        scale_one = rms_scale(rows_own)
        normed_one = rows_own * scale_one
        k["gain_one"] = jnp.sum(grad_hidden_one * normed_one, axis=0)
        k["rows"] = (
            grad_middle + norm_back(grad_hidden_one * gain_cols[:, 0], normed_one, scale_one)
        ).astype(BF16)
        k["attn"] = (hidden_one, grad_mixed, grad_forget, gated, output_in)
        kept.append(k)

    def joined(name, item):
        return jnp.concatenate([k[name][item] for k in kept])

    def total_of(name):
        return sum(k[name] for k in kept)

    grad_down = product_tn(joined("ffn", 0), joined("ffn", 1)).reshape(zs, 2, -1, width)
    down_share = unit_sum(grad_down, place.over_y, y_at)
    grad_ffn = product_tn(joined("ffn", 2), joined("ffn", 3))
    grad_ffn = grad_ffn.reshape(2, 2, zs, 2, own_rows, 2 * hidden).transpose(2, 3, 0, 1, 4, 5)
    ffn_sum = unit_sum(grad_ffn, place.over_y, y_at).reshape(4, own_rows, 2 * hidden)
    grad_out = product_tn(joined("attn", 3), joined("attn", 4)).reshape(zs, 2, own_rows, width)
    out_share = send(unit_sum(grad_out, place.over_x, x_at).astype(BF16), place.swap_xy).astype(F32)
    hidden_one_all = joined("attn", 0)
    grad_attn = product_tn(hidden_one_all, joined("attn", 1))
    grad_attn = grad_attn.reshape(2, 2, zs, 2, own_rows, 4 * part).transpose(2, 0, 3, 1, 4, 5)
    attn_sum = unit_sum(grad_attn, place.over_x, x_at).reshape(4, own_rows, 4 * part)

    ffn_low = ffn_sum.astype(BF16)
    ffn_share = exchange(
        lambda j: lax.dynamic_index_in_dim(ffn_low, j, 0, keepdims=False), at_x, x_perms
    )
    attn_low = attn_sum.astype(BF16)
    attn_share = exchange(
        lambda j: lax.dynamic_index_in_dim(attn_low, j, 0, keepdims=False), at_y, y_perms
    )

    def columns(shares, first, size):
        return jnp.concatenate([s[:, first : first + size] for s in shares], axis=1).astype(F32)

    grad_forgetw = product_tn(hidden_one_all, joined("attn", 2))
    small_grad = jnp.zeros((width, head_total + 4), F32)
    small_grad = lax.dynamic_update_slice(small_grad, grad_forgetw, (0, at_y * heads))
    zero = jnp.zeros((width,), F32)
    gain_grad = jnp.stack(
        [
            total_of("gain_one"),
            lax.dynamic_update_slice(zero, total_of("gain_query"), (at_y * part,)),
            lax.dynamic_update_slice(zero, total_of("gain_key"), (at_y * part,)),
            total_of("gain_three"),
        ],
        axis=1,
    )
    small_grad = small_grad.at[:, head_total:].set(gain_grad)
    small_share = lax.psum_scatter(small_grad, BOTH, scatter_dimension=0, tiled=True)
    bias_sum = lax.psum(
        lax.dynamic_update_slice(jnp.zeros((head_total,), F32), total_of("bias"), (at_y * heads,)),
        BOTH,
    )
    return (
        jnp.stack([k["result"] for k in kept]),
        jnp.stack([k["rows"] for k in kept]),
        columns(attn_share, 0, part),
        columns(attn_share, part, part),
        columns(attn_share, 2 * part, part),
        columns(attn_share, 3 * part, part),
        out_share,
        small_share[:, :head_total],
        bias_sum,
        small_share[:, head_total:],
        columns(ffn_share, 0, hidden),
        columns(ffn_share, hidden, hidden),
        down_share,
    )


def solution(mesh):
    place = Place(mesh)
    rows = P(BOTH, None)
    tokens = P(None, BOTH, None)
    in_specs = (tokens,) * 3 + (rows,) * 6 + (P(),) + (rows,) * 4
    out_specs = (tokens,) * 2 + (rows,) * 6 + (P(),) + (rows,) * 4

    def step(*args):
        return local(place, *args)

    return jax.shard_map(step, mesh=mesh, in_specs=in_specs, out_specs=out_specs, check_vma=False)
```
